32 devices in a mesh: row: 8 (over y, x, core), col: 4 (over z).
Axes of the slice: x: 2, y: 2, z: 4, core: 2. Of those that a mesh axis runs over, the one named last changes fastest.
Arguments:
- tokens: bfloat16 [8192, 5120], P('row'), may hold values from -6 to 6
- cotangent: bfloat16 [8192, 4096], P('row', 'col'), may hold values from -0.099609375 to 0.099609375
- small_weight: bfloat16 [2560, 4096], P(None, 'col'), may hold values from -0.125 to 0.125
- expand_in: bfloat16 [5120, 2560], P('row'), may hold values from -0.125 to 0.125
- expand_out: bfloat16 [4096, 4096], P('row', 'col'), may hold values from -0.09375 to 0.09375
Outputs:
- projected: bfloat16 [8192, 4096], P('row', 'col')
- grad_grown: float32 [5120, 4096], P('row', 'col')
- grad_in: float32 [5120, 2560], P('row', 'col')
- grad_out: float32 [4096, 4096], P('row', 'col')
The draws below stay inside these ranges and needn't reach their ends.
All inputs are finite; a program needn't handle non-finite values.
Results may differ from the reference program's by a relative error of at most 0.014.
Values may be sent and summed in bfloat16 or wider, within the bound.
A program may use at most 128 MiB of HBM per device.

```python
import jax
import jax.numpy as jnp
from jax import lax

DM = 5120
DS = 2560
QS = 4096
QL = 4096
TOKENS = 8192


def levels(key, extent, cuts, least, largest):
    def one(position, parts):
        heights = jax.random.uniform(jax.random.fold_in(jax.random.fold_in(key, 6), position), (parts,), jnp.float32, least / len(cuts), largest / len(cuts))
        return jnp.repeat(jnp.exp(heights), extent[position] // parts).reshape((-1,) + (1,) * (len(extent) - position - 1))

    level = one(*cuts[0])
    for cut in cuts[1:]:
        level = level * one(*cut)
    return level


def centred(stream_key, shape, deviation, most, pieces=(), held_as=jnp.bfloat16):
    factor_of = levels(stream_key, shape, pieces, -0.22, 0.18) if pieces else 1.0
    entries = jax.random.normal(stream_key, shape, jnp.float32) * deviation * factor_of
    return jnp.minimum(jnp.maximum(entries, -most), most).astype(held_as)


def setup_inputs(seed: int = 0) -> dict:
    splits = jax.random.split(jax.random.key(seed), 6)
    return {
        "tokens": centred(splits[0], (TOKENS, DM), 1.0, 6.0, ((0, 8),)),
        "cotangent": centred(splits[1], (TOKENS, QL), 0.015625, 0.099609375, ((0, 8), (1, 4))),
        "small_weight": centred(splits[2], (DS, QS), DS ** -0.5, 0.125, ((1, 4),)),
        "expand_in": centred(splits[3], (DM, DS), DS ** -0.5, 0.125, ((0, 8),)),
        "expand_out": centred(splits[4], (QS, QL), QS ** -0.5, 0.09375, ((0, 8), (1, 4))),
    }


def reference(tokens, cotangent, small_weight, expand_in, expand_out):
    mixed = jnp.dot(expand_in, small_weight, preferred_element_type=jnp.float32).astype(jnp.bfloat16)
    grown = jnp.dot(mixed, expand_out, preferred_element_type=jnp.float32).astype(jnp.bfloat16)
    projected = jnp.dot(tokens, grown, preferred_element_type=jnp.float32).astype(jnp.bfloat16)
    grad_grown = lax.dot_general(tokens, cotangent, (((0,), (0,)), ((), ())), preferred_element_type=jnp.float32)
    grad_low = grad_grown.astype(jnp.bfloat16)
    back = lax.dot_general(grad_low, expand_out, (((1,), (1,)), ((), ())), preferred_element_type=jnp.float32).astype(jnp.bfloat16)
    grad_in = lax.dot_general(back, small_weight, (((1,), (1,)), ((), ())), preferred_element_type=jnp.float32)
    grad_out = lax.dot_general(mixed, grad_low, (((0,), (0,)), ((), ())), preferred_element_type=jnp.float32)
    return projected, grad_grown, grad_in, grad_out
```

```python
import jax
import jax.numpy as jnp
from jax import lax
from jax.sharding import PartitionSpec as P

BF = jnp.bfloat16
F32 = jnp.float32


def dot(a, b, ca, cb):
    return lax.dot_general(a, b, (((ca,), (cb,)), ((), ())), preferred_element_type=F32)


def body(tokens, cotangent, small_weight, expand_in, expand_out):
    rows = lax.axis_size("row")
    r = lax.axis_index("row")
    band = small_weight.shape[0] // rows
    mine = lax.dynamic_slice_in_dim(small_weight, r * band, band, 0)
    small_rows = lax.all_gather(mine, "col", axis=1, tiled=True)
    out_panel = lax.all_gather(expand_out, "row", axis=0, tiled=True)
    grad_part = dot(tokens, cotangent, 0, 0).astype(BF)
    grad_sum = lax.psum_scatter(grad_part, "row", scatter_dimension=0, tiled=True)
    grad_grown = grad_sum.astype(F32)
    grad_low = grad_sum
    pair_part = dot(small_rows, out_panel, 1, 0).astype(BF)
    pair = lax.all_gather(pair_part, "row", axis=0, tiled=True)
    grown = dot(expand_in, pair, 1, 0).astype(BF)
    grown_all = lax.all_gather(grown, "row", axis=0, tiled=True)
    low_part = dot(expand_in, grad_low, 0, 0).astype(BF)
    low = lax.psum_scatter(low_part, "row", scatter_dimension=0, tiled=True)
    grad_in = lax.psum_scatter(
        dot(grad_low, pair, 1, 1).astype(BF), "col", scatter_dimension=1, tiled=True
    ).astype(F32)
    grad_out = lax.psum_scatter(
        dot(small_rows, low, 0, 0).astype(BF), "row", scatter_dimension=0, tiled=True
    ).astype(F32)
    projected = dot(tokens, grown_all, 1, 0).astype(BF)
    return (projected, grad_grown, grad_in, grad_out)


def solution(mesh):
    in_specs = (P("row", None), P("row", "col"), P(None, "col"), P("row", None), P("row", "col"))
    out_specs = (P("row", "col"), P("row", "col"), P("row", "col"), P("row", "col"))
    return jax.shard_map(body, mesh=mesh, in_specs=in_specs, out_specs=out_specs, check_vma=False)
```

```python
import functools

import jax
import jax.numpy as jnp
from jax import lax
from jax.experimental import pallas as pl
from jax.experimental.pallas import tpu as pltpu
from jax.sharding import PartitionSpec as P

BF = jnp.bfloat16
F32 = jnp.float32
TILE = 16
CHUNKS = 2


def dot(a, b, ca, cb):
    return lax.dot_general(a, b, (((ca,), (cb,)), ((), ())), preferred_element_type=F32)


def exchange_kernel(rows, gathers, scatters, *refs):
    na, nr = len(gathers), len(scatters)
    ag_in, rs_in = refs[:na], refs[na : na + nr]
    ag_out, rs_out = refs[na + nr : 2 * na + nr], refs[2 * na + nr : 2 * na + 2 * nr]
    scratch = refs[2 * na + 2 * nr :]
    bufs = [scratch[6 * i : 6 * i + 6] for i in range(nr)]
    send_sems, recv_sems, local_sems = scratch[6 * nr :]
    span = rows // 4
    r = lax.axis_index("row")
    core, b, a = r % 2, (r // 2) % 2, r // 4

    def index(j, db, dk):
        return ((a + j) % span * 2 + (b + db) % 2) * 2 + (core + dk) % 2

    sib, side = index(0, 0, 1), index(0, 1, 0)
    along = [index(j, 0, 0) for j in range(1, span)]
    behind = [index(span - j, 0, 0) for j in range(1, span)]
    corner = [index(span - j, 1, 0) for j in range(1, span)]

    barrier = pltpu.get_barrier_semaphore()
    for peer in [sib, side] + along:
        pl.semaphore_signal(
            barrier, inc=1, device_id={"row": peer}, device_id_type=pl.DeviceIdType.MESH
        )
    pl.semaphore_wait(barrier, span + 1)

    copies = []

    def push(src, dst, peer):
        i = len(copies)
        copy = pltpu.make_async_remote_copy(
            src_ref=src,
            dst_ref=dst,
            send_sem=send_sems.at[i],
            recv_sem=recv_sems.at[i],
            device_id={"row": peer},
            device_id_type=pl.DeviceIdType.MESH,
        )
        copy.start()
        copies.append(copy)
        return copy

    def at(block, n, start, size):
        return pl.ds(pl.multiple_of(block * n + start, 16), size)

    parts = []
    for i, (_, w) in enumerate(scatters):
        for c in range(CHUNKS):
            parts.append((i, pl.ds(c * (w // CHUNKS), w // CHUNKS)))

    first = []
    for i, cols in parts:
        n = scatters[i][0] // rows
        first.append(
            [
                push(
                    rs_in[i].at[at(index(q // 2, q % 2, 1), n, 0, n), cols],
                    bufs[i][0].at[q, :, cols],
                    sib,
                )
                for q in list(range(1, 2 * span)) + [0]
            ]
        )

    locals_ = []
    own = []
    for i, (n, _) in enumerate(gathers):
        h = n // 2
        x, o = ag_in[i], ag_out[i]
        copy = pltpu.make_async_copy(x, o.at[at(r, n, 0, n)], local_sems.at[i])
        copy.start()
        locals_.append(copy)
        b1 = push(x.at[pl.ds(0, h)], o.at[at(r, n, 0, h)], side)
        a2 = [push(x.at[pl.ds(h, h)], o.at[at(r, n, h, h)], p) for p in along]
        b2 = push(x.at[pl.ds(h, h)], o.at[at(r, n, h, h)], side)
        a1 = [push(x.at[pl.ds(0, h)], o.at[at(r, n, 0, h)], p) for p in along]
        s = push(x, o.at[at(r, n, 0, n)], sib)
        own.append((b1, a2, b2, a1, s))

    def add(size, store, *loads):
        def step(t):
            sl = pl.ds(pl.multiple_of(t * TILE, TILE), TILE)
            total = loads[0](sl).astype(F32)
            for load in loads[1:]:
                total = total + load(sl).astype(F32)
            store(sl, total)

        pl.loop(0, size // TILE)(step)

    def shift(sl, start):
        return pl.ds(pl.multiple_of(sl.start + start, TILE), TILE)

    hop1 = []
    for (i, cols), arrivals in zip(parts, first):
        n = scatters[i][0] // rows
        h = n // 2
        x = rs_in[i]
        sibs, acc, r1b, r1a, _, _ = bufs[i]
        for copy in arrivals:
            copy.wait_recv()
        for q in range(1, 2 * span):
            base = index(q // 2, q % 2, 0) * n

            def store(sl, total, q=q):
                acc[q, sl, cols] = total.astype(BF)

            add(
                n,
                store,
                lambda sl, base=base: x[shift(sl, base), cols],
                lambda sl, q=q: sibs[q, sl, cols],
            )
        tob = [
            push(acc.at[2 * j + 1, pl.ds(0, h), cols], r1b.at[j, :, cols], side)
            for j in range(span)
        ]
        toa = [
            [
                push(acc.at[2 * j + db, pl.ds(h, h), cols], r1a.at[j - 1, db, :, cols], along[j - 1])
                for db in range(2)
            ]
            for j in range(1, span)
        ]
        hop1.append((tob, toa))

    forward = []
    for i, (n, _) in enumerate(gathers):
        h = n // 2
        o = ag_out[i]
        b1, a2, b2, a1, s = own[i]
        b1.wait_recv()
        fa = [push(o.at[at(side, n, 0, h)], o.at[at(side, n, 0, h)], p) for p in along]
        fb = []
        for j in range(1, span):
            a2[j - 1].wait_recv()
            rows_in = at(behind[j - 1], n, h, h)
            fb.append(push(o.at[rows_in], o.at[rows_in], side))
        forward.append((fa, fb))

    hop2 = []
    for (i, cols), (tob, toa) in zip(parts, hop1):
        n = scatters[i][0] // rows
        h = n // 2
        _, acc, r1b, r1a, r2a, r2b = bufs[i]
        for copy in tob:
            copy.wait_recv()
        toa2 = []
        for j in range(1, span):

            def store(sl, total, j=j):
                acc[2 * j, sl, cols] = total.astype(BF)

            add(h, store, lambda sl, j=j: acc[2 * j, sl, cols], lambda sl, j=j: r1b[j, sl, cols])
            toa2.append(push(acc.at[2 * j, pl.ds(0, h), cols], r2a.at[j - 1, :, cols], along[j - 1]))
        for pair in toa:
            for copy in pair:
                copy.wait_recv()

        def store2(sl, total):
            acc[1, shift(sl, h), cols] = total.astype(BF)

        add(
            h,
            store2,
            lambda sl: acc[1, shift(sl, h), cols],
            *[lambda sl, j=j: r1a[j - 1, 1, sl, cols] for j in range(1, span)],
        )
        tob2 = push(acc.at[1, pl.ds(h, h), cols], r2b.at[:, cols], side)
        hop2.append((toa2, tob2))

    share = []
    for i, (n, _) in enumerate(gathers):
        o = ag_out[i]
        b1, a2, b2, a1, s = own[i]
        b2.wait_recv()
        blk = at(side, n, 0, n)
        share.append(push(o.at[blk], o.at[blk], sib))
        for j in range(1, span):
            a1[j - 1].wait_recv()
            blk = at(behind[j - 1], n, 0, n)
            share.append(push(o.at[blk], o.at[blk], sib))

    for (i, cols), (toa2, tob2) in zip(parts, hop2):
        n = scatters[i][0] // rows
        h = n // 2
        x, out = rs_in[i], rs_out[i]
        sibs, acc, r1b, r1a, r2a, r2b = bufs[i]
        for copy in toa2:
            copy.wait_recv()
        base = r * n

        def store1(sl, total):
            out[sl, cols] = total

        add(
            h,
            store1,
            lambda sl: x[shift(sl, base), cols],
            lambda sl: sibs[0, sl, cols],
            lambda sl: r1b[0, sl, cols],
            *[lambda sl, j=j: r2a[j - 1, sl, cols] for j in range(1, span)],
        )
        tob2.wait_recv()

        def store2(sl, total):
            out[shift(sl, h), cols] = total

        add(
            h,
            store2,
            lambda sl: x[shift(sl, base + h), cols],
            lambda sl: sibs[0, shift(sl, h), cols],
            *[lambda sl, j=j: r1a[j - 1, 0, sl, cols] for j in range(1, span)],
            lambda sl: r2b[sl, cols],
        )

    for i, (n, _) in enumerate(gathers):
        o = ag_out[i]
        fa, fb = forward[i]
        for j in range(1, span):
            fa[j - 1].wait_recv()
            fb[j - 1].wait_recv()
            blk = at(corner[j - 1], n, 0, n)
            share.append(push(o.at[blk], o.at[blk], sib))
    for group in own:
        group[4].wait_recv()
    for copy in share:
        copy.wait_recv()
    for copy in locals_:
        copy.wait()
    for copy in copies:
        copy.wait_send()


def exchange(rows, name, collective_id, gather, scatter):
    span = rows // 4
    gathers = [x.shape for x in gather]
    scatters = [x.shape for x in scatter]
    scratch = []
    for m, w in scatters:
        n = m // rows
        h = n // 2
        scratch += [
            pltpu.VMEM((2 * span, n, w), BF),
            pltpu.VMEM((2 * span, n, w), BF),
            pltpu.VMEM((span, h, w), BF),
            pltpu.VMEM((span - 1, 2, h, w), BF),
            pltpu.VMEM((span - 1, h, w), BF),
            pltpu.VMEM((h, w), BF),
        ]
    count = CHUNKS * len(scatters) * (6 * span - 2) + len(gathers) * (6 * span - 2)
    scratch += [
        pltpu.SemaphoreType.DMA((count,)),
        pltpu.SemaphoreType.DMA((count,)),
        pltpu.SemaphoreType.DMA((max(1, len(gathers)),)),
    ]
    moved = sum(m * w * 2 * rows for m, w in gathers) + sum(m * w * 2 for m, w in scatters)
    any_, vmem = pl.BlockSpec(memory_space=pl.ANY), pl.BlockSpec(memory_space=pltpu.VMEM)
    return pl.pallas_call(
        functools.partial(exchange_kernel, rows, gathers, scatters),
        out_shape=[jax.ShapeDtypeStruct((m * rows, w), BF) for m, w in gathers]
        + [jax.ShapeDtypeStruct((m // rows, w), F32) for m, w in scatters],
        in_specs=[any_] * len(gathers) + [vmem] * len(scatters),
        out_specs=[any_] * len(gathers) + [vmem] * len(scatters),
        scratch_shapes=scratch,
        compiler_params=pltpu.CompilerParams(
            collective_id=collective_id, has_side_effects=True, vmem_limit_bytes=48 * 1024 * 1024
        ),
        cost_estimate=pl.CostEstimate(flops=0, bytes_accessed=10 * moved, transcendentals=0),
        name=name,
    )(*gather, *scatter)


def body(tokens, cotangent, small_weight, expand_in, expand_out):
    rows = lax.axis_size("row")
    r = lax.axis_index("row")
    band = small_weight.shape[0] // rows
    mine = lax.dynamic_slice_in_dim(small_weight, r * band, band, 0)
    small_rows = lax.all_gather(mine, "col", axis=1, tiled=True)
    grad_part = dot(tokens, cotangent, 0, 0).astype(BF)
    out_panel, grad_grown = exchange(rows, "grad_grown", 1, [expand_out], [grad_part])
    grad_low = grad_grown.astype(BF)
    pair_part = dot(small_rows, out_panel, 1, 0).astype(BF)
    low_part = dot(expand_in, grad_low, 0, 0).astype(BF)
    pair, low = exchange(rows, "pair", 2, [pair_part], [low_part])
    low = low.astype(BF)
    grad_in = lax.psum_scatter(
        dot(grad_low, pair, 1, 1).astype(BF), "col", scatter_dimension=1, tiled=True
    ).astype(F32)
    grown = dot(expand_in, pair, 1, 0).astype(BF)
    out_part = dot(small_rows, low, 0, 0).astype(BF)
    grown_all, grad_out = exchange(rows, "grad_out", 3, [grown], [out_part])
    projected = dot(tokens, grown_all, 1, 0).astype(BF)
    return (projected, grad_grown, grad_in, grad_out)


def solution(mesh):
    in_specs = (P("row", None), P("row", "col"), P(None, "col"), P("row", None), P("row", "col"))
    out_specs = (P("row", "col"), P("row", "col"), P("row", "col"), P("row", "col"))
    return jax.shard_map(body, mesh=mesh, in_specs=in_specs, out_specs=out_specs, check_vma=False)
```

```python
import functools

import jax
import jax.numpy as jnp
from jax import lax
from jax.experimental import pallas as pl
from jax.experimental.pallas import tpu as pltpu
from jax.sharding import PartitionSpec as P

BF = jnp.bfloat16
F32 = jnp.float32
TILE = 16
CHUNKS = 2


def dot(a, b, ca, cb):
    return lax.dot_general(a, b, (((ca,), (cb,)), ((), ())), preferred_element_type=F32)


def exchange_kernel(rows, gathers, scatters, make, use, *refs):
    na, nr = len(gathers), len(scatters)
    refs = list(refs)

    def take(count):
        taken, refs[:] = refs[:count], refs[count:]
        return taken

    ag_in = take(na)
    rs_in = take(0 if make else nr)
    tokens = take(1)[0] if make or use else None
    cotangent = take(1)[0] if make else None
    ag_out = take(0 if use else na)
    rs_out = take(nr)
    product = take(1)[0] if use else None
    if make or use:
        held, held_sem = take(2)
    if make:
        held_cot, terms = take(2)
        rs_in = [terms]
    if use:
        whole, total = take(2)
        ag_out = [whole]
    scratch = refs
    bufs = [scratch[6 * i : 6 * i + 6] for i in range(nr)]
    send_sems, recv_sems, local_sems = scratch[6 * nr :]
    span = rows // 4
    r = lax.axis_index("row")
    core, b, a = r % 2, (r // 2) % 2, r // 4

    def index(j, db, dk):
        return ((a + j) % span * 2 + (b + db) % 2) * 2 + (core + dk) % 2

    sib, side = index(0, 0, 1), index(0, 1, 0)
    along = [index(j, 0, 0) for j in range(1, span)]
    behind = [index(span - j, 0, 0) for j in range(1, span)]
    corner = [index(span - j, 1, 0) for j in range(1, span)]

    barrier = pltpu.get_barrier_semaphore()
    for peer in [sib, side] + along:
        pl.semaphore_signal(
            barrier, inc=1, device_id={"row": peer}, device_id_type=pl.DeviceIdType.MESH
        )
    pl.semaphore_wait(barrier, span + 1)

    copies = []

    def push(src, dst, peer):
        i = len(copies)
        copy = pltpu.make_async_remote_copy(
            src_ref=src,
            dst_ref=dst,
            send_sem=send_sems.at[i],
            recv_sem=recv_sems.at[i],
            device_id={"row": peer},
            device_id_type=pl.DeviceIdType.MESH,
        )
        copy.start()
        copies.append(copy)
        return copy

    def at(block, n, start, size):
        return pl.ds(pl.multiple_of(block * n + start, 16), size)

    if make or use:
        fetch = pltpu.make_async_copy(tokens, held, held_sem.at[0])
        fetch.start()
    if make:
        fetch_cot = pltpu.make_async_copy(cotangent, held_cot, held_sem.at[1])
        fetch_cot.start()
    parts = []
    for i, (_, w) in enumerate(scatters):
        for c in range(CHUNKS):
            parts.append((i, pl.ds(c * (w // CHUNKS), w // CHUNKS)))

    def add(size, store, *loads):
        def step(t):
            sl = pl.ds(pl.multiple_of(t * TILE, TILE), TILE)
            total = loads[0](sl).astype(F32)
            for load in loads[1:]:
                total = total + load(sl).astype(F32)
            store(sl, total)

        pl.loop(0, size // TILE)(step)

    def shift(sl, start):
        return pl.ds(pl.multiple_of(sl.start + start, TILE), TILE)

    def multiply(q):
        if not use:
            return
        n = gathers[0][0]
        start = pl.multiple_of(index(q // 2, q % 2, 0) // 2 * 2 * n, 128)
        height = min(256, tokens.shape[0])

        def tile(t):
            sl = pl.ds(pl.multiple_of(t * height, TILE), height)
            term = dot(held[sl, pl.ds(start, 2 * n)], whole[pl.ds(start, 2 * n), :], 1, 0)
            if q == 0:
                total[sl, :] = term
            elif q == 2 * span - 1:
                product[sl, :] = (total[sl, :] + term).astype(BF)
            else:
                total[sl, :] += term

        pl.loop(0, tokens.shape[0] // height)(tile)

    def send_terms():
        first = []
        for i, cols in parts:
            n = scatters[i][0] // rows
            first.append(
                [
                    push(
                        rs_in[i].at[at(index(q // 2, q % 2, 1), n, 0, n), cols],
                        bufs[i][0].at[q, :, cols],
                        sib,
                    )
                    for q in list(range(1, 2 * span)) + [0]
                ]
            )

        return first

    if not make:
        first = send_terms()

    locals_ = []
    own = []
    for i, (n, _) in enumerate(gathers):
        h = n // 2
        x, o = ag_in[i], ag_out[i]
        copy = pltpu.make_async_copy(x, o.at[at(r, n, 0, n)], local_sems.at[i])
        copy.start()
        locals_.append(copy)
        b1 = push(x.at[pl.ds(0, h)], o.at[at(r, n, 0, h)], side)
        a2 = [push(x.at[pl.ds(h, h)], o.at[at(r, n, h, h)], p) for p in along]
        b2 = push(x.at[pl.ds(h, h)], o.at[at(r, n, h, h)], side)
        a1 = [push(x.at[pl.ds(0, h)], o.at[at(r, n, 0, h)], p) for p in along]
        s = push(x, o.at[at(r, n, 0, n)], sib)
        own.append((b1, a2, b2, a1, s))

    if make:
        n = scatters[0][0] // rows
        width = 2 * n if n % 128 else n
        fetch.wait()
        fetch_cot.wait()
        first = [[] for _ in parts]
        for q in list(range(1, 2 * span)) + [0]:
            chip = index(q // 2, q % 2, 0) // 2

            def tile(t):
                start = pl.multiple_of(chip * 2 * n + t * width, 128)
                terms[pl.ds(start, width), :] = dot(
                    held[:, pl.ds(start, width)], held_cot[...], 0, 0
                ).astype(BF)

            pl.loop(0, 2 * n // width)(tile)
            for (_, cols), group in zip(parts, first):
                rows_out = at(index(q // 2, q % 2, 1), n, 0, n)
                group.append(push(terms.at[rows_out, cols], bufs[0][0].at[q, :, cols], sib))

    def hop_one():
        hop1 = []
        for (i, cols), arrivals in zip(parts, first):
            n = scatters[i][0] // rows
            h = n // 2
            x = rs_in[i]
            sibs, acc, r1b, r1a, _, _ = bufs[i]
            for copy in arrivals:
                copy.wait_recv()
            for q in range(1, 2 * span):
                base = index(q // 2, q % 2, 0) * n

                def store(sl, total, q=q):
                    acc[q, sl, cols] = total.astype(BF)

                add(
                    n,
                    store,
                    lambda sl, base=base: x[shift(sl, base), cols],
                    lambda sl, q=q: sibs[q, sl, cols],
                )
            tob = [
                push(acc.at[2 * j + 1, pl.ds(0, h), cols], r1b.at[j, :, cols], side)
                for j in range(span)
            ]
            toa = [
                [
                    push(acc.at[2 * j + db, pl.ds(h, h), cols], r1a.at[j - 1, db, :, cols], along[j - 1])
                    for db in range(2)
                ]
                for j in range(1, span)
            ]
            hop1.append((tob, toa))

        return hop1

    def hop_gather():
        forward = []
        for i, (n, _) in enumerate(gathers):
            h = n // 2
            o = ag_out[i]
            b1, a2, b2, a1, s = own[i]
            b1.wait_recv()
            fa = [push(o.at[at(side, n, 0, h)], o.at[at(side, n, 0, h)], p) for p in along]
            fb = []
            for j in range(1, span):
                a2[j - 1].wait_recv()
                rows_in = at(behind[j - 1], n, h, h)
                fb.append(push(o.at[rows_in], o.at[rows_in], side))
            forward.append((fa, fb))

        return forward

    if make:
        forward = hop_gather()
        hop1 = hop_one()
    else:
        hop1 = hop_one()
        forward = hop_gather()
    if use:
        fetch.wait()
        own[0][4].wait_recv()
        locals_[0].wait()
        multiply(0)

    hop2 = []
    for (i, cols), (tob, toa) in zip(parts, hop1):
        n = scatters[i][0] // rows
        h = n // 2
        _, acc, r1b, r1a, r2a, r2b = bufs[i]
        for copy in tob:
            copy.wait_recv()
        toa2 = []
        for j in range(1, span):

            def store(sl, total, j=j):
                acc[2 * j, sl, cols] = total.astype(BF)

            add(h, store, lambda sl, j=j: acc[2 * j, sl, cols], lambda sl, j=j: r1b[j, sl, cols])
            toa2.append(push(acc.at[2 * j, pl.ds(0, h), cols], r2a.at[j - 1, :, cols], along[j - 1]))
        for pair in toa:
            for copy in pair:
                copy.wait_recv()

        def store2(sl, total):
            acc[1, shift(sl, h), cols] = total.astype(BF)

        add(
            h,
            store2,
            lambda sl: acc[1, shift(sl, h), cols],
            *[lambda sl, j=j: r1a[j - 1, 1, sl, cols] for j in range(1, span)],
        )
        tob2 = push(acc.at[1, pl.ds(h, h), cols], r2b.at[:, cols], side)
        hop2.append((toa2, tob2))

    share = []
    for i, (n, _) in enumerate(gathers):
        o = ag_out[i]
        b1, a2, b2, a1, s = own[i]
        b2.wait_recv()
        blk = at(side, n, 0, n)
        share.append(push(o.at[blk], o.at[blk], sib))
        for j in range(1, span):
            a1[j - 1].wait_recv()
            blk = at(behind[j - 1], n, 0, n)
            share.append(push(o.at[blk], o.at[blk], sib))

    shared = list(share)
    if use:
        for copy in shared:
            copy.wait_recv()
        for q in [1] + [2 * j for j in range(1, span)]:
            multiply(q)

    for (i, cols), (toa2, tob2) in zip(parts, hop2):
        n = scatters[i][0] // rows
        h = n // 2
        x, out = rs_in[i], rs_out[i]
        sibs, acc, r1b, r1a, r2a, r2b = bufs[i]
        for copy in toa2:
            copy.wait_recv()
        base = r * n

        def store1(sl, total):
            out[sl, cols] = total

        add(
            h,
            store1,
            lambda sl: x[shift(sl, base), cols],
            lambda sl: sibs[0, sl, cols],
            lambda sl: r1b[0, sl, cols],
            *[lambda sl, j=j: r2a[j - 1, sl, cols] for j in range(1, span)],
        )
        tob2.wait_recv()

        def store2(sl, total):
            out[shift(sl, h), cols] = total

        add(
            h,
            store2,
            lambda sl: x[shift(sl, base + h), cols],
            lambda sl: sibs[0, shift(sl, h), cols],
            *[lambda sl, j=j: r1a[j - 1, 0, sl, cols] for j in range(1, span)],
            lambda sl: r2b[sl, cols],
        )

    for i, (n, _) in enumerate(gathers):
        o = ag_out[i]
        fa, fb = forward[i]
        for j in range(1, span):
            fa[j - 1].wait_recv()
            fb[j - 1].wait_recv()
            blk = at(corner[j - 1], n, 0, n)
            share.append(push(o.at[blk], o.at[blk], sib))
    if not use:
        for group in own:
            group[4].wait_recv()
        for copy in shared:
            copy.wait_recv()
        for copy in locals_:
            copy.wait()
    for copy in share[len(shared) :]:
        copy.wait_recv()
    for j in range(1, span):
        multiply(2 * j + 1)
    for copy in copies:
        copy.wait_send()


def exchange(rows, name, collective_id, gather, scatter, make=None, use=None):
    span = rows // 4
    gathers = [x.shape for x in gather]
    scatters = [(make[0].shape[1], make[1].shape[1])] if make else [x.shape for x in scatter]
    extra = list(make) if make else [use] if use is not None else []
    scratch = []
    if extra:
        scratch += [pltpu.VMEM(extra[0].shape, BF), pltpu.SemaphoreType.DMA((2,))]
    if make:
        scratch += [pltpu.VMEM(make[1].shape, BF), pltpu.VMEM(scatters[0], BF)]
    products = []
    if use is not None:
        (n, w), m = gathers[0], use.shape[0]
        scratch += [pltpu.VMEM((rows * n, w), BF), pltpu.VMEM((m, w), F32)]
        products = [jax.ShapeDtypeStruct((m, w), BF)]
    kept = 0 if use is not None else len(gathers)
    for m, w in scatters:
        n = m // rows
        h = n // 2
        scratch += [
            pltpu.VMEM((2 * span, n, w), BF),
            pltpu.VMEM((2 * span, n, w), BF),
            pltpu.VMEM((span, h, w), BF),
            pltpu.VMEM((span - 1, 2, h, w), BF),
            pltpu.VMEM((span - 1, h, w), BF),
            pltpu.VMEM((h, w), BF),
        ]
    count = CHUNKS * len(scatters) * (6 * span - 2) + len(gathers) * (6 * span - 2)
    scratch += [
        pltpu.SemaphoreType.DMA((count,)),
        pltpu.SemaphoreType.DMA((count,)),
        pltpu.SemaphoreType.DMA((max(1, len(gathers)),)),
    ]
    moved = sum(m * w * 2 * rows for m, w in gathers) + sum(m * w * 2 for m, w in scatters)
    any_, vmem = pl.BlockSpec(memory_space=pl.ANY), pl.BlockSpec(memory_space=pltpu.VMEM)
    return pl.pallas_call(
        functools.partial(
            exchange_kernel, rows, gathers, scatters, make is not None, use is not None
        ),
        out_shape=[jax.ShapeDtypeStruct((m * rows, w), BF) for m, w in gathers[:kept]]
        + [jax.ShapeDtypeStruct((m // rows, w), F32) for m, w in scatters]
        + products,
        in_specs=[any_] * len(gathers) + [vmem] * len(scatter) + [any_] * len(extra),
        out_specs=[any_] * kept + [vmem] * (len(scatters) + len(products)),
        scratch_shapes=scratch,
        compiler_params=pltpu.CompilerParams(
            collective_id=collective_id, has_side_effects=True, vmem_limit_bytes=58 * 1024 * 1024
        ),
        cost_estimate=pl.CostEstimate(flops=0, bytes_accessed=10 * moved, transcendentals=0),
        name=name,
    )(*gather, *scatter, *extra)


def body(tokens, cotangent, small_weight, expand_in, expand_out):
    rows = lax.axis_size("row")
    r = lax.axis_index("row")
    band = small_weight.shape[0] // rows
    mine = lax.dynamic_slice_in_dim(small_weight, r * band, band, 0)
    small_rows = lax.all_gather(mine, "col", axis=1, tiled=True)
    out_panel, grad_grown = exchange(
        rows, "grad_grown", 1, [expand_out], [], make=(tokens, cotangent)
    )
    grad_low = grad_grown.astype(BF)
    pair_part = dot(small_rows, out_panel, 1, 0).astype(BF)
    low_part = dot(expand_in, grad_low, 0, 0).astype(BF)
    pair, low = exchange(rows, "pair", 2, [pair_part], [low_part])
    low = low.astype(BF)
    grad_in = lax.psum_scatter(
        dot(grad_low, pair, 1, 1).astype(BF), "col", scatter_dimension=1, tiled=True
    ).astype(F32)
    grown = dot(expand_in, pair, 1, 0).astype(BF)
    out_part = dot(small_rows, low, 0, 0).astype(BF)
    grad_out, projected = exchange(rows, "grad_out", 3, [grown], [out_part], use=tokens)
    return (projected, grad_grown, grad_in, grad_out)


def solution(mesh):
    in_specs = (P("row", None), P("row", "col"), P(None, "col"), P("row", None), P("row", "col"))
    out_specs = (P("row", "col"), P("row", "col"), P("row", "col"), P("row", "col"))
    return jax.shard_map(body, mesh=mesh, in_specs=in_specs, out_specs=out_specs, check_vma=False)
```
